32 devices in a mesh: frames: 2 (over y), wide: 4 (over z), narrow: 4 (over x, core).
Axes of the slice: x: 2, y: 2, z: 4, core: 2. Of those that a mesh axis runs over, the one named last changes fastest.
Arguments:
- slc: bfloat16 [2, 16, 80, 5120], P(None, ('frames', 'wide'), 'narrow'), parts along dimension 1, may hold values from -6 to 6
- pair_list: int32 [16, 2], replicated, may hold values from 0 to 7, as said below
- owner: int32 [16], replicated, may hold values from 0 to 15, each once
Outputs:
- interferogram: float32 [2, 32, 16, 256], P(None, ('frames', 'wide'), 'narrow'), parts along dimension 1
- coherence: float32 [32, 16, 256], P(('frames', 'wide'), 'narrow'), parts along dimension 0
The draws below stay inside these ranges and needn't reach their ends.
There are 2 independent parts, one for each index of `frames`. The reference program is written for one: setup_inputs(seed, part) draws one part's arguments, and reference() takes and returns one part's arrays. A program takes and returns all parts, laid end to end along the dimension named above; an argument that names none is the same for every part. Nothing has to cross between parts.
Inputs may be any that keep to these rules, and one draw needn't show every extreme that they name: `pair_list`: each row holds a reference date and a strictly later secondary date at most 6 dates after it; no two rows are equal; dates are unevenly used, earlier ones more often.
All inputs are finite; a program needn't handle non-finite values.
Results may differ from the reference program's by a relative error of at most 0.0003.
Values may be sent and summed in bfloat16 or wider, within the bound.
A program may use at most 128 MiB of HBM per device.

```python
import jax
import jax.numpy as jnp
from jax import lax

LCOLS = 256
ML_ROWS = 5
ML_COLS = 20
DATES = 8
PAIRS = 16
LROWS = 16
ROWS = 80
COLS = 5120


def draw_pair_list(key, part):
    key = jax.random.fold_in(key, 11)
    count = DATES * 6
    index = jnp.arange(count, dtype=jnp.int32)
    refdate = index // 6
    gap = index % 6 + 1
    valid = refdate + gap <= DATES - 1
    noise = jax.random.randint(key, (count,), 0, 4096)
    bias = (DATES - 1 - refdate) * 2048 // DATES
    score = jnp.where(valid, noise + bias, -8192)
    first_pair = (refdate == 0) & (gap == 1)
    last_pair = (refdate == DATES - 2) & (gap == 1)
    score = jnp.where(first_pair | last_pair, 8192, score)
    distinct = score * count + index
    picked = lax.top_k(distinct, PAIRS)[1].astype(jnp.int32)
    chosen_ref = picked // 6
    chosen_sec = chosen_ref + picked % 6 + 1
    return jnp.stack([chosen_ref, chosen_sec], axis=-1).astype(jnp.int32)


def level_of(rng, shape, shards, smallest, high):
    factor_of = 1.0
    for dim, parts in shards:
        heights = jax.random.uniform(jax.random.fold_in(jax.random.fold_in(rng, 6), dim), (parts,), jnp.float32, smallest / len(shards), high / len(shards))
        factor_of = factor_of * jnp.repeat(jnp.exp(heights), shape[dim] // parts).reshape((-1,) + (1,) * (len(shape) - 1 - dim))
    return factor_of


def centred(own_key, dims, deviation, bound, split=(), kind=jnp.bfloat16):
    level = level_of(own_key, dims, split, -0.22, 0.18) if split else 1.0
    drawn = jax.random.normal(own_key, dims, jnp.float32) * deviation * level
    return jnp.minimum(jnp.maximum(drawn, -bound), bound).astype(kind)


def setup_inputs(seed: int = 0, part: int = 0) -> dict:
    keys = jax.random.split(jax.random.key(seed), 4)
    own_keys = jax.random.split(jax.random.fold_in(keys[3], part), 4)
    return {
        "slc": centred(own_keys[0], (2, DATES, ROWS, COLS), 1.0, 6.0, ((1, 4), (2, 4))),
        "pair_list": draw_pair_list(jax.random.fold_in(keys[3], 71), part),
        "owner": jax.random.permutation(keys[2], PAIRS).astype(jnp.int32),
    }


def cross_terms(first, second):
    a0 = first[0].astype(jnp.float32)
    a1 = first[1].astype(jnp.float32)
    b0 = second[0].astype(jnp.float32)
    b1 = second[1].astype(jnp.float32)
    return jnp.stack([a0 * b0 + a1 * b1, a1 * b0 - a0 * b1, a0 * a0 + a1 * a1, b0 * b0 + b1 * b1])

def pair_looks(slc, chosen):
    first = lax.dynamic_index_in_dim(slc, chosen[0], 1, keepdims=False)
    second = lax.dynamic_index_in_dim(slc, chosen[1], 1, keepdims=False)
    terms = cross_terms(first, second)
    return terms.reshape(4, LROWS, ML_ROWS, LCOLS, ML_COLS).sum(axis=(2, 4))

def reference(slc, pair_list, owner):
    chosen = pair_list[owner]
    looked = lax.map(lambda item: pair_looks(slc, item), chosen)
    looked = jnp.transpose(looked, (1, 0, 2, 3))
    padded = jnp.pad(looked, ((0, 0), (0, 0), (1, 1), (1, 1)))
    rowsum = padded[:, :, :-2] + padded[:, :, 1:-1] + padded[:, :, 2:]
    boxed = rowsum[:, :, :, :-2] + rowsum[:, :, :, 1:-1] + rowsum[:, :, :, 2:]
    magnitude = jnp.sqrt(boxed[0] * boxed[0] + boxed[1] * boxed[1])
    coherence = magnitude / jnp.sqrt(boxed[2] * boxed[3] + 1e-06)
    interferogram = looked[:2] / (ML_ROWS * ML_COLS)
    return (interferogram, coherence)
```

```python
import functools

import jax
import jax.numpy as jnp
from jax import lax
from jax.experimental import pallas as pl
from jax.experimental.pallas import tpu as pltpu
from jax.sharding import PartitionSpec as P

PAIR_DEV = 4
ML_ROWS = 5
ML_COLS = 20


def with_halo(block, sides, width):
    for axis, dim in sides:
        count = lax.axis_size(axis)
        forward = [(i, i + 1) for i in range(count - 1)]
        backward = [(target, source) for source, target in forward]
        low = lax.ppermute(
            lax.slice_in_dim(block, block.shape[dim] - width, None, axis=dim), axis, forward
        )
        high = lax.ppermute(lax.slice_in_dim(block, 0, width, axis=dim), axis, backward)
        block = jnp.concatenate([low, block, high], axis=dim)
    return block


def cross_terms(first, second):
    a0 = first[0].astype(jnp.float32)
    a1 = first[1].astype(jnp.float32)
    b0 = second[0].astype(jnp.float32)
    b1 = second[1].astype(jnp.float32)
    return jnp.stack([a0 * b0 + a1 * b1, a1 * b0 - a0 * b1, a0 * a0 + a1 * a1, b0 * b0 + b1 * b1])


def gathered(slc, pair_list, owner):
    pair_dev = PAIR_DEV
    look_rows = slc.shape[2] // ML_ROWS
    slots = lax.dynamic_slice_in_dim(owner, lax.axis_index("wide") * pair_dev, pair_dev)
    chosen = pair_list[slots]
    needed = jnp.concatenate([chosen[:, 0], chosen[:, 1]])
    piece = lax.all_gather(slc, "wide", axis=1, tiled=True)
    count = piece.shape[1]
    onehot = (needed[:, None] == jnp.arange(count, dtype=jnp.int32)[None, :]).astype(jnp.bfloat16)
    picked = jnp.einsum("sp,cprk->csrk", onehot, piece, preferred_element_type=jnp.float32)
    selected = picked.astype(jnp.bfloat16)
    terms = cross_terms(selected[:, :pair_dev], selected[:, pair_dev:])
    band = terms.shape[3]
    looked = terms.reshape(4, pair_dev, look_rows, ML_ROWS, band // ML_COLS, ML_COLS).sum(
        axis=(3, 5)
    )
    padded = with_halo(looked, (("narrow", 2),), 1)
    rowsum = padded[:, :, :-2] + padded[:, :, 1:-1] + padded[:, :, 2:]
    rowsum = jnp.pad(rowsum, ((0, 0), (0, 0), (0, 0), (1, 1)))
    boxed = rowsum[:, :, :, :-2] + rowsum[:, :, :, 1:-1] + rowsum[:, :, :, 2:]
    magnitude = jnp.sqrt(boxed[0] * boxed[0] + boxed[1] * boxed[1])
    coherence = magnitude / jnp.sqrt(boxed[2] * boxed[3] + 1e-06)
    interferogram = looked[:2] / (ML_ROWS * ML_COLS)
    return (interferogram, coherence)


LANES = 128


def split_terms(value):
    high = value.astype(jnp.bfloat16)
    return high, (value - high.astype(jnp.float32)).astype(jnp.bfloat16)


def exchange_kernel(
    wide, narrow, half, widths, pair_ref, owner_ref, slc_ref, inter_ref, coh_ref,
    pixels, stage, send_a, send_b, recv_a, recv_b, high_a, low_a, high_b, low_b,
    looks, message, edges, got, got_edges, grown,
    load_sem, send_sem, recv_sem, back_send, back_recv, edge_send, edge_recv,
):
    me = lax.axis_index("wide")
    row = lax.axis_index("narrow")
    above = lax.rem(row + narrow - 1, narrow)
    below = lax.rem(row + 1, narrow)
    if wide == 4:
        targets = [lax.rem(me + 2, wide), wide - 1 - me, me + 1 - 2 * lax.rem(me, 2), me]
    else:
        targets = [lax.rem(me + k, wide) for k in range(1, wide + 1)]
    others = targets[:-1]
    sends, recvs = (send_a, send_b), (recv_a, recv_b)
    dates = recv_a.shape[0]
    pairs = owner_ref.shape[0]
    look_rows = slc_ref.shape[2] // ML_ROWS

    load = pltpu.make_async_copy(slc_ref, pixels, load_sem)
    load.start()
    barrier = pltpu.get_barrier_semaphore()
    for target in others:
        pl.semaphore_signal(barrier, inc=1, device_id={"wide": target})
    for target in targets:
        for side in (above, below):
            pl.semaphore_signal(barrier, inc=1, device_id={"wide": target, "narrow": side})
    load.wait()

    def pack(target, part, dst):
        width = widths[part]
        offset = sum(widths[:part])
        for date in range(2):
            for comp in range(2):
                for group in range(2):
                    column = pl.multiple_of(target * (2 * half) + (group * half + offset), LANES)
                    block = pixels[comp, date, :, pl.ds(column, width)]
                    for tile in range(width // LANES):
                        stage[date, comp * 2 + group, tile, 0:20] = block[
                            :, tile * LANES : (tile + 1) * LANES
                        ].astype(jnp.float32)
            for line in range(ML_ROWS):
                for tile in range(width // LANES):
                    rows = [
                        stage[date, i, tile, pl.ds(line, look_rows, stride=ML_ROWS)]
                        for i in range(4)
                    ]
                    dst[date, line, :, tile * LANES : (tile + 1) * LANES] = jnp.concatenate(
                        rows, axis=0
                    ).astype(jnp.bfloat16)

    started = []
    for part in range(2):
        for k, target in enumerate(others):
            pack(target, part, sends[part].at[k])
            if part == 0 and k == 0:
                pl.semaphore_wait(barrier, 3 * wide - 1)
            copy = pltpu.make_async_remote_copy(
                src_ref=sends[part].at[k],
                dst_ref=recvs[part].at[pl.ds(2 * me, 2)],
                send_sem=send_sem.at[part, k],
                recv_sem=recv_sem.at[part, me],
                device_id={"wide": target},
            )
            copy.start()
            started.append(copy)
    for part in range(2):
        pack(me, part, recvs[part].at[pl.ds(2 * me, 2)])

    looks_half = half // ML_COLS

    def work(part):
        width = widths[part]
        offset = sum(widths[:part])
        recv = recvs[part]
        high, low = ((high_a, low_a), (high_b, low_b))[part]
        pixel = lax.broadcasted_iota(jnp.int32, (width, LANES), 0) + offset
        look = lax.broadcasted_iota(jnp.int32, (width, LANES), 1) & (looks_half - 1)
        first = look * ML_COLS
        summer = ((pixel >= first) & (pixel < first + ML_COLS)).astype(jnp.bfloat16)

        for k, target in enumerate(others):
            pltpu.make_async_remote_copy(
                src_ref=sends[part].at[k],
                dst_ref=recv.at[pl.ds(2 * target, 2)],
                send_sem=send_sem.at[part, k],
                recv_sem=recv_sem.at[part, target],
                device_id={"wide": target},
            ).wait_recv()

        def power(i, carry):
            both = []
            for date in range(2):
                total = jnp.zeros((8, width), jnp.float32)
                for line in range(ML_ROWS):
                    value = recv[2 * i + date, line].astype(jnp.float32)
                    total += value[:8] * value[:8] + value[8:] * value[8:]
                both.append(total)
            high[pairs + i], low[pairs + i] = split_terms(jnp.concatenate(both, axis=0))
            return carry

        lax.fori_loop(0, dates // 2, power, 0)

        def cross(slot, carry):
            chosen = owner_ref[slot]
            one, two = pair_ref[chosen, 0], pair_ref[chosen, 1]
            real = jnp.zeros((8, width), jnp.float32)
            imag = jnp.zeros((8, width), jnp.float32)
            for line in range(ML_ROWS):
                a = recv[one, line].astype(jnp.float32)
                b = recv[two, line].astype(jnp.float32)
                real += a[:8] * b[:8] + a[8:] * b[8:]
                imag += a[8:] * b[:8] - a[:8] * b[8:]
            high[slot], low[slot] = split_terms(jnp.concatenate([real, imag], axis=0))
            return carry

        lax.fori_loop(0, pairs, cross, 0)
        count = high.shape[0] * 16
        summed = jnp.dot(
            high[...].reshape(count, width), summer, preferred_element_type=jnp.float32
        ) + jnp.dot(low[...].reshape(count, width), summer, preferred_element_type=jnp.float32)
        summed = summed.reshape(count // 8, 8, LANES)
        if part == 0:
            looks[...] = summed
        else:
            looks[...] += summed

    work(0)
    work(1)

    sub = lax.broadcasted_iota(jnp.int32, (8, LANES), 0)
    lane = lax.broadcasted_iota(jnp.int32, (8, LANES), 1)
    low_half = sub < 4
    left = lane < 64
    group_zero = (lane & 32) == 0
    back = []
    for k, target in enumerate(targets):
        own = k == wide - 1
        for term in range(4):
            held = jnp.zeros((8, LANES), jnp.float32)
            for slot in range(PAIR_DEV):
                place = target * PAIR_DEV + slot
                if term < 2:
                    value = looks[2 * place + term]
                else:
                    value = looks[2 * pairs + pair_ref[owner_ref[place], term - 2]]
                turned = pltpu.roll(value, 4, 0)
                if slot < 2:
                    value = jnp.where(group_zero, value, turned)
                else:
                    value = jnp.where(group_zero, turned, value)
                here = (low_half if slot < 2 else ~low_half) & (left if slot % 2 == 0 else ~left)
                held = jnp.where(here, value, held)
            message[k, 8 * term : 8 * term + 8] = held
        for side in range(2):
            edges[k, side] = message[k, pl.ds(3 * side, 8, stride=4)]
        if own:
            got[me] = message[k]
        else:
            copy = pltpu.make_async_remote_copy(
                src_ref=message.at[k],
                dst_ref=got.at[me],
                send_sem=back_send.at[k],
                recv_sem=back_recv.at[me],
                device_id={"wide": target},
            )
            copy.start()
            back.append(copy)
        for side in range(2):
            copy = pltpu.make_async_remote_copy(
                src_ref=edges.at[k, side],
                dst_ref=got_edges.at[side, me],
                send_sem=edge_send.at[side, k],
                recv_sem=edge_recv.at[side, me],
                device_id={"wide": target, "narrow": (above, below)[side]},
            )
            copy.start()
            back.append(copy)

    for copy in started:
        copy.wait_send()
    for k, target in enumerate(targets):
        if k < wide - 1:
            pltpu.make_async_remote_copy(
                src_ref=message.at[k],
                dst_ref=got.at[target],
                send_sem=back_send.at[k],
                recv_sem=back_recv.at[target],
                device_id={"wide": target},
            ).wait_recv()
        for side in range(2):
            pltpu.make_async_remote_copy(
                src_ref=edges.at[k, side],
                dst_ref=got_edges.at[side, target],
                send_sem=edge_send.at[side, k],
                recv_sem=edge_recv.at[side, target],
                device_id={"wide": target, "narrow": (above, below)[side]},
            ).wait_recv()

    def across(parts, parity):
        tiles = []
        for i in range(0, wide, 2):
            one, two = parts[i], parts[i + 1]
            if parity == 0:
                tiles.append(jnp.where(left, one, pltpu.roll(two, 64, 1)))
            else:
                tiles.append(jnp.where(left, pltpu.roll(one, 64, 1), two))
        return jnp.concatenate(tiles, axis=1)

    for parity in range(2):
        top = across([got_edges[1, w] for w in range(wide)], parity)
        bottom = across([got_edges[0, w] for w in range(wide)], parity)
        top = jnp.where(row == 0, 0.0, top)
        bottom = jnp.where(row == narrow - 1, 0.0, bottom)
        for term in range(4):
            middle = across([got[w, 8 * term : 8 * term + 8] for w in range(wide)], parity)
            for upper in range(2):
                slot = 2 * upper + parity
                edge = 2 * term + upper
                grown[term, slot, 0:1] = top[edge : edge + 1]
                grown[term, slot, 1:5] = middle[4 * upper : 4 * upper + 4]
                grown[term, slot, 5:6] = bottom[edge : edge + 1]

    columns = wide * 64
    place = lax.broadcasted_iota(jnp.int32, (4, columns), 1)
    for slot in range(PAIR_DEV):
        boxed = []
        for term in range(4):
            rows = grown[term, slot, 0:4] + grown[term, slot, 1:5] + grown[term, slot, 2:6]
            before = jnp.where(place == 0, 0.0, pltpu.roll(rows, 1, 1))
            after = jnp.where(place == columns - 1, 0.0, pltpu.roll(rows, columns - 1, 1))
            boxed.append(before + rows + after)
            if term < 2:
                inter_ref[term, slot] = grown[term, slot, 1:5] / (ML_ROWS * ML_COLS)
        magnitude = jnp.sqrt(boxed[0] * boxed[0] + boxed[1] * boxed[1])
        coh_ref[slot] = magnitude / jnp.sqrt(boxed[2] * boxed[3] + 1e-06)

    for copy in back:
        copy.wait_send()


def exchanged(slc, pair_list, owner):
    wide = lax.axis_size("wide")
    narrow = lax.axis_size("narrow")
    columns = slc.shape[3]
    half = columns // wide // 2
    first = half // 2 // LANES * LANES
    widths = (first, half - first)
    pairs = owner.shape[0]
    dates = 2 * wide
    blocks = pairs + dates // 2
    bf16, f32 = jnp.bfloat16, jnp.float32
    scratch = [
        pltpu.VMEM(slc.shape, bf16),
        pltpu.VMEM((2, 4, widths[1] // LANES, 24, LANES), f32),
    ]
    scratch += [pltpu.VMEM((wide - 1, 2, ML_ROWS, 16, n), bf16) for n in widths]
    scratch += [pltpu.VMEM((dates, ML_ROWS, 16, n), bf16) for n in widths]
    scratch += [pltpu.VMEM((blocks, 16, n), bf16) for n in widths for _ in range(2)]
    scratch += [
        pltpu.VMEM((2 * blocks, 8, LANES), f32),
        pltpu.VMEM((wide, 32, LANES), f32),
        pltpu.VMEM((wide, 2, 8, LANES), f32),
        pltpu.VMEM((wide, 32, LANES), f32),
        pltpu.VMEM((2, wide, 8, LANES), f32),
        pltpu.VMEM((4, PAIR_DEV, 8, wide * 64), f32),
        pltpu.SemaphoreType.DMA,
        pltpu.SemaphoreType.DMA((2, wide - 1)),
        pltpu.SemaphoreType.DMA((2, wide)),
        pltpu.SemaphoreType.DMA((wide,)),
        pltpu.SemaphoreType.DMA((wide,)),
        pltpu.SemaphoreType.DMA((2, wide)),
        pltpu.SemaphoreType.DMA((2, wide)),
    ]
    look_rows = slc.shape[2] // ML_ROWS
    look_columns = columns // ML_COLS
    return pl.pallas_call(
        functools.partial(exchange_kernel, wide, narrow, half, widths),
        out_shape=(
            jax.ShapeDtypeStruct((2, PAIR_DEV, look_rows, look_columns), f32),
            jax.ShapeDtypeStruct((PAIR_DEV, look_rows, look_columns), f32),
        ),
        in_specs=[
            pl.BlockSpec(memory_space=pltpu.SMEM),
            pl.BlockSpec(memory_space=pltpu.SMEM),
            pl.BlockSpec(memory_space=pl.ANY),
        ],
        out_specs=(pl.BlockSpec(memory_space=pltpu.VMEM), pl.BlockSpec(memory_space=pltpu.VMEM)),
        scratch_shapes=scratch,
        compiler_params=pltpu.CompilerParams(
            collective_id=0, has_side_effects=True, vmem_limit_bytes=32 * 1024 * 1024
        ),
    )(pair_list, owner, slc)


def solution(mesh):
    in_specs = (P(None, ("frames", "wide"), "narrow", None), P(), P())
    out_specs = (P(None, ("frames", "wide"), "narrow", None), P(("frames", "wide"), "narrow", None))

    def on_device(slc, pair_list, owner):
        wide, narrow = mesh.shape["wide"], mesh.shape["narrow"]
        tiled = slc.shape[3] == wide * 2 * ML_COLS * 32
        if tiled and narrow > 2 and wide % 2 == 0 and slc.shape[1:3] == (2, 4 * ML_ROWS):
            return exchanged(slc, pair_list, owner)
        return gathered(slc, pair_list, owner)

    return jax.shard_map(
        on_device, mesh=mesh, in_specs=in_specs, out_specs=out_specs, check_vma=False
    )
```

```python
import functools

import jax
import jax.numpy as jnp
from jax import lax
from jax.experimental import pallas as pl
from jax.experimental.pallas import tpu as pltpu
from jax.sharding import PartitionSpec as P

PAIR_DEV = 4
ML_ROWS = 5
ML_COLS = 20


def with_halo(block, sides, width):
    for axis, dim in sides:
        count = lax.axis_size(axis)
        forward = [(i, i + 1) for i in range(count - 1)]
        backward = [(target, source) for source, target in forward]
        low = lax.ppermute(
            lax.slice_in_dim(block, block.shape[dim] - width, None, axis=dim), axis, forward
        )
        high = lax.ppermute(lax.slice_in_dim(block, 0, width, axis=dim), axis, backward)
        block = jnp.concatenate([low, block, high], axis=dim)
    return block


def cross_terms(first, second):
    a0 = first[0].astype(jnp.float32)
    a1 = first[1].astype(jnp.float32)
    b0 = second[0].astype(jnp.float32)
    b1 = second[1].astype(jnp.float32)
    return jnp.stack([a0 * b0 + a1 * b1, a1 * b0 - a0 * b1, a0 * a0 + a1 * a1, b0 * b0 + b1 * b1])


def gathered(slc, pair_list, owner):
    pair_dev = PAIR_DEV
    look_rows = slc.shape[2] // ML_ROWS
    slots = lax.dynamic_slice_in_dim(owner, lax.axis_index("wide") * pair_dev, pair_dev)
    chosen = pair_list[slots]
    needed = jnp.concatenate([chosen[:, 0], chosen[:, 1]])
    piece = lax.all_gather(slc, "wide", axis=1, tiled=True)
    count = piece.shape[1]
    onehot = (needed[:, None] == jnp.arange(count, dtype=jnp.int32)[None, :]).astype(jnp.bfloat16)
    picked = jnp.einsum("sp,cprk->csrk", onehot, piece, preferred_element_type=jnp.float32)
    selected = picked.astype(jnp.bfloat16)
    terms = cross_terms(selected[:, :pair_dev], selected[:, pair_dev:])
    band = terms.shape[3]
    looked = terms.reshape(4, pair_dev, look_rows, ML_ROWS, band // ML_COLS, ML_COLS).sum(
        axis=(3, 5)
    )
    padded = with_halo(looked, (("narrow", 2),), 1)
    rowsum = padded[:, :, :-2] + padded[:, :, 1:-1] + padded[:, :, 2:]
    rowsum = jnp.pad(rowsum, ((0, 0), (0, 0), (0, 0), (1, 1)))
    boxed = rowsum[:, :, :, :-2] + rowsum[:, :, :, 1:-1] + rowsum[:, :, :, 2:]
    magnitude = jnp.sqrt(boxed[0] * boxed[0] + boxed[1] * boxed[1])
    coherence = magnitude / jnp.sqrt(boxed[2] * boxed[3] + 1e-06)
    interferogram = looked[:2] / (ML_ROWS * ML_COLS)
    return (interferogram, coherence)


LANES = 128
PART = 256
WINDOW = 9


def split_terms(value):
    high = value.astype(jnp.bfloat16)
    return high, (value - high.astype(jnp.float32)).astype(jnp.bfloat16)


def exchange_kernel(
    wide, narrow, half, widths, window, pair_ref, owner_ref, slc_ref, inter_ref, coh_ref,
    pixels, stage, sends, recvs, highs, lows, looks, message, edges, got, got_edges, grown,
    load_sem, send_sem, recv_sem, back_send, back_recv, edge_send, edge_recv,
):
    me = lax.axis_index("wide")
    row = lax.axis_index("narrow")
    above = lax.rem(row + narrow - 1, narrow)
    below = lax.rem(row + 1, narrow)
    if wide == 4:
        targets = [lax.rem(me + 2, wide), wide - 1 - me, me + 1 - 2 * lax.rem(me, 2), me]
    else:
        targets = [lax.rem(me + k, wide) for k in range(1, wide + 1)]
    others = targets[:-1]
    dates = recvs[0].shape[0]
    parts = len(widths)
    pairs = owner_ref.shape[0]
    lines = slc_ref.shape[1]
    look_rows = lines // ML_ROWS

    loads = []
    for k, target in enumerate(targets):
        band = pl.ds(pl.multiple_of(target * (2 * half), LANES), 2 * half)
        load = pltpu.make_async_copy(
            slc_ref.at[:, :, :, band], pixels.at[:, :, :, band], load_sem.at[k]
        )
        load.start()
        loads.append(load)
    barrier = pltpu.get_barrier_semaphore()
    for target in others:
        pl.semaphore_signal(barrier, inc=1, device_id={"wide": target})
    for target in targets:
        for side in (above, below):
            pl.semaphore_signal(barrier, inc=1, device_id={"wide": target, "narrow": side})

    def pack(target, part, dst):
        width = widths[part]
        offset = sum(widths[:part])
        for comp in range(2):
            for group in range(2):
                column = pl.multiple_of(target * (2 * half) + (group * half + offset), LANES)
                for line in range(lines):
                    block = pixels[comp, line, :, pl.ds(column, width)].astype(jnp.float32)
                    for tile in range(width // LANES):
                        stage[comp * 2 + group, tile, 2 * line : 2 * line + 2] = block[
                            :, tile * LANES : (tile + 1) * LANES
                        ]
        for date in range(2):
            for line in range(ML_ROWS):
                for tile in range(width // LANES):
                    rows = [
                        stage[i, tile, pl.ds(2 * line + date, look_rows, stride=2 * ML_ROWS)]
                        for i in range(4)
                    ]
                    dst[date, line, :, tile * LANES : (tile + 1) * LANES] = jnp.concatenate(
                        rows, axis=0
                    ).astype(jnp.bfloat16)

    started = []

    def send(part):
        for k, target in enumerate(others):
            if part == 0:
                loads[k].wait()
            pack(target, part, sends[part].at[k])
            if part == 0 and k == 0:
                pl.semaphore_wait(barrier, 3 * wide - 1)
            copy = pltpu.make_async_remote_copy(
                src_ref=sends[part].at[k],
                dst_ref=recvs[part].at[pl.ds(2 * me, 2)],
                send_sem=send_sem.at[part, k],
                recv_sem=recv_sem.at[part, me],
                device_id={"wide": target},
            )
            copy.start()
            started.append(copy)

    for part in range(min(window, parts)):
        send(part)
    loads[-1].wait()
    for part in range(parts):
        pack(me, part, recvs[part].at[pl.ds(2 * me, 2)])

    looks_half = half // ML_COLS

    def work(part):
        width = widths[part]
        offset = sum(widths[:part])
        recv = recvs[part]
        high, low = highs[part], lows[part]
        pixel = lax.broadcasted_iota(jnp.int32, (width, LANES), 0) + offset
        look = lax.broadcasted_iota(jnp.int32, (width, LANES), 1) & (looks_half - 1)
        first = look * ML_COLS
        summer = ((pixel >= first) & (pixel < first + ML_COLS)).astype(jnp.bfloat16)

        for k, target in enumerate(others):
            pltpu.make_async_remote_copy(
                src_ref=sends[part].at[k],
                dst_ref=recv.at[pl.ds(2 * target, 2)],
                send_sem=send_sem.at[part, k],
                recv_sem=recv_sem.at[part, target],
                device_id={"wide": target},
            ).wait_recv()

        def power(i, carry):
            both = []
            for date in range(2):
                total = jnp.zeros((8, width), jnp.float32)
                for line in range(ML_ROWS):
                    value = recv[2 * i + date, line].astype(jnp.float32)
                    total += value[:8] * value[:8] + value[8:] * value[8:]
                both.append(total)
            high[pairs + i], low[pairs + i] = split_terms(jnp.concatenate(both, axis=0))
            return carry

        lax.fori_loop(0, dates // 2, power, 0, unroll=2)

        def cross(slot, carry):
            chosen = owner_ref[slot]
            one, two = pair_ref[0, chosen], pair_ref[1, chosen]
            real = jnp.zeros((8, width), jnp.float32)
            imag = jnp.zeros((8, width), jnp.float32)
            for line in range(ML_ROWS):
                a = recv[one, line].astype(jnp.float32)
                b = recv[two, line].astype(jnp.float32)
                real += a[:8] * b[:8] + a[8:] * b[8:]
                imag += a[8:] * b[:8] - a[:8] * b[8:]
            high[slot], low[slot] = split_terms(jnp.concatenate([real, imag], axis=0))
            return carry

        lax.fori_loop(0, pairs, cross, 0, unroll=4)
        count = high.shape[0] * 16
        summed = jnp.dot(
            high[...].reshape(count, width), summer, preferred_element_type=jnp.float32
        ) + jnp.dot(low[...].reshape(count, width), summer, preferred_element_type=jnp.float32)
        summed = summed.reshape(count // 8, 8, LANES)
        if part == 0:
            looks[...] = summed
        else:
            looks[...] += summed

    for part in range(parts):
        if part + window < parts:
            for copy in started[part * len(others) : (part + 1) * len(others)]:
                copy.wait_send()
            send(part + window)
        work(part)

    sub = lax.broadcasted_iota(jnp.int32, (8, LANES), 0)
    lane = lax.broadcasted_iota(jnp.int32, (8, LANES), 1)
    low_half = sub < 4
    left = lane < 64
    group_zero = (lane & 32) == 0
    back = []
    for k, target in enumerate(targets):
        own = k == wide - 1
        for term in range(4):
            held = jnp.zeros((8, LANES), jnp.float32)
            for slot in range(PAIR_DEV):
                place = target * PAIR_DEV + slot
                if term < 2:
                    value = looks[2 * place + term]
                else:
                    value = looks[2 * pairs + pair_ref[term - 2, owner_ref[place]]]
                turned = pltpu.roll(value, 4, 0)
                if slot < 2:
                    value = jnp.where(group_zero, value, turned)
                else:
                    value = jnp.where(group_zero, turned, value)
                here = (low_half if slot < 2 else ~low_half) & (left if slot % 2 == 0 else ~left)
                held = jnp.where(here, value, held)
            message[k, 8 * term : 8 * term + 8] = held
        for side in range(2):
            edges[k, side] = message[k, pl.ds(3 * side, 8, stride=4)]
        if own:
            got[me] = message[k]
        else:
            copy = pltpu.make_async_remote_copy(
                src_ref=message.at[k],
                dst_ref=got.at[me],
                send_sem=back_send.at[k],
                recv_sem=back_recv.at[me],
                device_id={"wide": target},
            )
            copy.start()
            back.append(copy)
        for side in range(2):
            copy = pltpu.make_async_remote_copy(
                src_ref=edges.at[k, side],
                dst_ref=got_edges.at[side, me],
                send_sem=edge_send.at[side, k],
                recv_sem=edge_recv.at[side, me],
                device_id={"wide": target, "narrow": (above, below)[side]},
            )
            copy.start()
            back.append(copy)

    for copy in started[max(parts - window, 0) * len(others) :]:
        copy.wait_send()
    for k, target in enumerate(targets):
        if k < wide - 1:
            pltpu.make_async_remote_copy(
                src_ref=message.at[k],
                dst_ref=got.at[target],
                send_sem=back_send.at[k],
                recv_sem=back_recv.at[target],
                device_id={"wide": target},
            ).wait_recv()
        for side in range(2):
            pltpu.make_async_remote_copy(
                src_ref=edges.at[k, side],
                dst_ref=got_edges.at[side, target],
                send_sem=edge_send.at[side, k],
                recv_sem=edge_recv.at[side, target],
                device_id={"wide": target, "narrow": (above, below)[side]},
            ).wait_recv()

    def across(parts, parity):
        tiles = []
        for i in range(0, wide, 2):
            one, two = parts[i], parts[i + 1]
            if parity == 0:
                tiles.append(jnp.where(left, one, pltpu.roll(two, 64, 1)))
            else:
                tiles.append(jnp.where(left, pltpu.roll(one, 64, 1), two))
        return jnp.concatenate(tiles, axis=1)

    for parity in range(2):
        top = across([got_edges[1, w] for w in range(wide)], parity)
        bottom = across([got_edges[0, w] for w in range(wide)], parity)
        top = jnp.where(row == 0, 0.0, top)
        bottom = jnp.where(row == narrow - 1, 0.0, bottom)
        for term in range(4):
            middle = across([got[w, 8 * term : 8 * term + 8] for w in range(wide)], parity)
            for upper in range(2):
                slot = 2 * upper + parity
                edge = 2 * term + upper
                grown[term, slot, 0:1] = top[edge : edge + 1]
                grown[term, slot, 1:5] = middle[4 * upper : 4 * upper + 4]
                grown[term, slot, 5:6] = bottom[edge : edge + 1]

    columns = wide * 64
    place = lax.broadcasted_iota(jnp.int32, (4, columns), 1)
    for slot in range(PAIR_DEV):
        boxed = []
        for term in range(4):
            rows = grown[term, slot, 0:4] + grown[term, slot, 1:5] + grown[term, slot, 2:6]
            before = jnp.where(place == 0, 0.0, pltpu.roll(rows, 1, 1))
            after = jnp.where(place == columns - 1, 0.0, pltpu.roll(rows, columns - 1, 1))
            boxed.append(before + rows + after)
            if term < 2:
                inter_ref[term, slot] = grown[term, slot, 1:5] / (ML_ROWS * ML_COLS)
        magnitude = jnp.sqrt(boxed[0] * boxed[0] + boxed[1] * boxed[1])
        coh_ref[slot] = magnitude / jnp.sqrt(boxed[2] * boxed[3] + 1e-06)

    for copy in back:
        copy.wait_send()


def exchanged(slc, pair_list, owner):
    wide = lax.axis_size("wide")
    narrow = lax.axis_size("narrow")
    columns = slc.shape[3]
    half = columns // wide // 2
    widths = tuple(min(PART, half - i) for i in range(0, half, PART))
    pairs = owner.shape[0]
    dates = 2 * wide
    blocks = pairs + dates // 2
    bf16, f32 = jnp.bfloat16, jnp.float32
    scratch = [
        pltpu.VMEM((2, slc.shape[2], 2, columns), bf16),
        pltpu.VMEM((4, widths[0] // LANES, 2 * slc.shape[2], LANES), f32),
    ]
    scratch += [
        [pltpu.VMEM((wide - 1, 2, ML_ROWS, 16, n), bf16) for n in widths],
        [pltpu.VMEM((dates, ML_ROWS, 16, n), bf16) for n in widths],
        [pltpu.VMEM((blocks, 16, n), bf16) for n in widths],
        [pltpu.VMEM((blocks, 16, n), bf16) for n in widths],
    ]
    scratch += [
        pltpu.VMEM((2 * blocks, 8, LANES), f32),
        pltpu.VMEM((wide, 32, LANES), f32),
        pltpu.VMEM((wide, 2, 8, LANES), f32),
        pltpu.VMEM((wide, 32, LANES), f32),
        pltpu.VMEM((2, wide, 8, LANES), f32),
        pltpu.VMEM((4, PAIR_DEV, 8, wide * 64), f32),
        pltpu.SemaphoreType.DMA((wide,)),
        pltpu.SemaphoreType.DMA((len(widths), wide - 1)),
        pltpu.SemaphoreType.DMA((len(widths), wide)),
        pltpu.SemaphoreType.DMA((wide,)),
        pltpu.SemaphoreType.DMA((wide,)),
        pltpu.SemaphoreType.DMA((2, wide)),
        pltpu.SemaphoreType.DMA((2, wide)),
    ]
    look_rows = slc.shape[2] // ML_ROWS
    look_columns = columns // ML_COLS
    return pl.pallas_call(
        functools.partial(exchange_kernel, wide, narrow, half, widths, WINDOW),
        out_shape=(
            pltpu.VMEM((2, PAIR_DEV, look_rows, look_columns), f32),
            pltpu.VMEM((PAIR_DEV, look_rows, look_columns), f32),
        ),
        in_specs=[
            pl.BlockSpec(memory_space=pltpu.SMEM),
            pl.BlockSpec(memory_space=pltpu.SMEM),
            pl.BlockSpec(memory_space=pltpu.HBM),
        ],
        out_specs=(pl.BlockSpec(memory_space=pltpu.VMEM), pl.BlockSpec(memory_space=pltpu.VMEM)),
        scratch_shapes=scratch,
        compiler_params=pltpu.CompilerParams(
            collective_id=0, has_side_effects=True, vmem_limit_bytes=56 * 1024 * 1024
        ),
    )(*(pltpu.with_memory_space_constraint(x, pltpu.HBM) for x in (pair_list.T, owner, slc.transpose(0, 2, 1, 3))))


def solution(mesh):
    in_specs = (P(None, ("frames", "wide"), "narrow", None), P(), P())
    out_specs = (P(None, ("frames", "wide"), "narrow", None), P(("frames", "wide"), "narrow", None))

    def on_device(slc, pair_list, owner):
        wide, narrow = mesh.shape["wide"], mesh.shape["narrow"]
        tiled = slc.shape[3] == wide * 2 * ML_COLS * 32
        if tiled and narrow > 2 and wide % 2 == 0 and slc.shape[1:3] == (2, 4 * ML_ROWS):
            return exchanged(slc, pair_list, owner)
        return gathered(slc, pair_list, owner)

    return jax.shard_map(
        on_device, mesh=mesh, in_specs=in_specs, out_specs=out_specs, check_vma=False
    )
```

```python
import functools

import jax
import jax.numpy as jnp
from jax import lax
from jax.experimental import pallas as pl
from jax.experimental.pallas import tpu as pltpu
from jax.sharding import PartitionSpec as P

PAIR_DEV = 4
ML_ROWS = 5
ML_COLS = 20


def with_halo(block, sides, width):
    for axis, dim in sides:
        count = lax.axis_size(axis)
        forward = [(i, i + 1) for i in range(count - 1)]
        backward = [(target, source) for source, target in forward]
        low = lax.ppermute(
            lax.slice_in_dim(block, block.shape[dim] - width, None, axis=dim), axis, forward
        )
        high = lax.ppermute(lax.slice_in_dim(block, 0, width, axis=dim), axis, backward)
        block = jnp.concatenate([low, block, high], axis=dim)
    return block


def cross_terms(first, second):
    a0 = first[0].astype(jnp.float32)
    a1 = first[1].astype(jnp.float32)
    b0 = second[0].astype(jnp.float32)
    b1 = second[1].astype(jnp.float32)
    return jnp.stack([a0 * b0 + a1 * b1, a1 * b0 - a0 * b1, a0 * a0 + a1 * a1, b0 * b0 + b1 * b1])


def gathered(slc, pair_list, owner):
    pair_dev = PAIR_DEV
    look_rows = slc.shape[2] // ML_ROWS
    slots = lax.dynamic_slice_in_dim(owner, lax.axis_index("wide") * pair_dev, pair_dev)
    chosen = pair_list[slots]
    needed = jnp.concatenate([chosen[:, 0], chosen[:, 1]])
    piece = lax.all_gather(slc, "wide", axis=1, tiled=True)
    count = piece.shape[1]
    onehot = (needed[:, None] == jnp.arange(count, dtype=jnp.int32)[None, :]).astype(jnp.bfloat16)
    picked = jnp.einsum("sp,cprk->csrk", onehot, piece, preferred_element_type=jnp.float32)
    selected = picked.astype(jnp.bfloat16)
    terms = cross_terms(selected[:, :pair_dev], selected[:, pair_dev:])
    band = terms.shape[3]
    looked = terms.reshape(4, pair_dev, look_rows, ML_ROWS, band // ML_COLS, ML_COLS).sum(
        axis=(3, 5)
    )
    padded = with_halo(looked, (("narrow", 2),), 1)
    rowsum = padded[:, :, :-2] + padded[:, :, 1:-1] + padded[:, :, 2:]
    rowsum = jnp.pad(rowsum, ((0, 0), (0, 0), (0, 0), (1, 1)))
    boxed = rowsum[:, :, :, :-2] + rowsum[:, :, :, 1:-1] + rowsum[:, :, :, 2:]
    magnitude = jnp.sqrt(boxed[0] * boxed[0] + boxed[1] * boxed[1])
    coherence = magnitude / jnp.sqrt(boxed[2] * boxed[3] + 1e-06)
    interferogram = looked[:2] / (ML_ROWS * ML_COLS)
    return (interferogram, coherence)


LANES = 128
PART = 256


def split_terms(value):
    high = value.astype(jnp.bfloat16)
    return high, (value - high.astype(jnp.float32)).astype(jnp.bfloat16)


def exchange_kernel(
    wide, narrow, half, widths, pair_ref, owner_ref, slc_ref, inter_ref, coh_ref,
    pixels, stage, sends, recvs, highs, lows, looks, message, edges, got, got_edges,
    own_power, own_rims, power, rims, grown, below_line,
    load_sem, send_sem, recv_sem, back_send, back_recv, edge_send, edge_recv,
    power_send, power_recv, rim_send, rim_recv,
):
    me = lax.axis_index("wide")
    row = lax.axis_index("narrow")
    above = lax.rem(row + narrow - 1, narrow)
    below = lax.rem(row + 1, narrow)
    targets = [lax.rem(me + 2, wide), wide - 1 - me, me + 1 - 2 * lax.rem(me, 2), me]
    others = targets[:-1]
    parts = len(widths)
    pairs = owner_ref.shape[0]
    lines = slc_ref.shape[1]
    look_rows = lines // ML_ROWS

    loads = []
    for k, target in enumerate(targets):
        band = pl.ds(pl.multiple_of(target * (2 * half), LANES), 2 * half)
        load = pltpu.make_async_copy(
            slc_ref.at[:, :, :, band], pixels.at[:, :, :, band], load_sem.at[k]
        )
        load.start()
        loads.append(load)
    barrier = pltpu.get_barrier_semaphore()
    for target in others:
        pl.semaphore_signal(barrier, inc=1, device_id={"wide": target})
    for target in targets:
        for side in (above, below):
            pl.semaphore_signal(barrier, inc=1, device_id={"wide": target, "narrow": side})

    def pack(target, part, dst):
        width = widths[part]
        offset = sum(widths[:part])
        for comp in range(2):
            for group in range(2):
                column = pl.multiple_of(target * (2 * half) + (group * half + offset), LANES)
                for line in range(lines):
                    block = pixels[comp, line, :, pl.ds(column, width)].astype(jnp.float32)
                    for tile in range(width // LANES):
                        stage[comp * 2 + group, tile, 2 * line : 2 * line + 2] = block[
                            :, tile * LANES : (tile + 1) * LANES
                        ]
        for date in range(2):
            for line in range(ML_ROWS):
                for tile in range(width // LANES):
                    rows = [
                        stage[i, tile, pl.ds(2 * line + date, look_rows, stride=2 * ML_ROWS)]
                        for i in range(4)
                    ]
                    dst[date, line, :, tile * LANES : (tile + 1) * LANES] = jnp.concatenate(
                        rows, axis=0
                    ).astype(jnp.bfloat16)

    started = []

    def send(part):
        for k, target in enumerate(others):
            if part == 0:
                loads[k].wait()
            pack(target, part, sends[part].at[k])
            if part == 0 and k == 0:
                pl.semaphore_wait(barrier, 3 * wide - 1)
            copy = pltpu.make_async_remote_copy(
                src_ref=sends[part].at[k],
                dst_ref=recvs[part].at[pl.ds(2 * me, 2)],
                send_sem=send_sem.at[part, k],
                recv_sem=recv_sem.at[part, me],
                device_id={"wide": target},
            )
            copy.start()
            started.append(copy)

    for part in range(parts):
        send(part)
    loads[-1].wait()
    for part in range(parts):
        pack(me, part, recvs[part].at[pl.ds(2 * me, 2)])

    looks_half = half // ML_COLS

    def summer(part):
        width = widths[part]
        offset = sum(widths[:part])
        pixel = lax.broadcasted_iota(jnp.int32, (width, LANES), 0) + offset
        look = lax.broadcasted_iota(jnp.int32, (width, LANES), 1) & (looks_half - 1)
        first = look * ML_COLS
        return ((pixel >= first) & (pixel < first + ML_COLS)).astype(jnp.bfloat16)

    def add_looks(part, begin, end):
        width = widths[part]
        count = (end - begin) * 16
        spread = summer(part)
        summed = jnp.dot(
            highs[part][begin:end].reshape(count, width),
            spread,
            preferred_element_type=jnp.float32,
        ) + jnp.dot(
            lows[part][begin:end].reshape(count, width),
            spread,
            preferred_element_type=jnp.float32,
        )
        summed = summed.reshape(count // 8, 8, LANES)
        if part == 0:
            looks[2 * begin : 2 * end] = summed
        else:
            looks[2 * begin : 2 * end] += summed

    def powers(part):
        width = widths[part]
        for k in range(wide):
            both = []
            for date in range(2):
                total = jnp.zeros((8, width), jnp.float32)
                for line in range(ML_ROWS):
                    if k < wide - 1:
                        value = sends[part][k, date, line].astype(jnp.float32)
                    else:
                        value = recvs[part][2 * me + date, line].astype(jnp.float32)
                    total += value[:8] * value[:8] + value[8:] * value[8:]
                both.append(total)
            highs[part][pairs + k], lows[part][pairs + k] = split_terms(
                jnp.concatenate(both, axis=0)
            )
        add_looks(part, pairs, pairs + wide)

    def work(part):
        width = widths[part]
        recv = recvs[part]
        high, low = highs[part], lows[part]
        for k, target in enumerate(others):
            pltpu.make_async_remote_copy(
                src_ref=sends[part].at[k],
                dst_ref=recv.at[pl.ds(2 * target, 2)],
                send_sem=send_sem.at[part, k],
                recv_sem=recv_sem.at[part, target],
                device_id={"wide": target},
            ).wait_recv()

        def cross(slot, carry):
            chosen = owner_ref[slot]
            one, two = pair_ref[0, chosen], pair_ref[1, chosen]
            real = jnp.zeros((8, width), jnp.float32)
            imag = jnp.zeros((8, width), jnp.float32)
            for line in range(ML_ROWS):
                a = recv[one, line].astype(jnp.float32)
                b = recv[two, line].astype(jnp.float32)
                real += a[:8] * b[:8] + a[8:] * b[8:]
                imag += a[8:] * b[:8] - a[:8] * b[8:]
            high[slot], low[slot] = split_terms(jnp.concatenate([real, imag], axis=0))
            return carry

        lax.fori_loop(0, pairs, cross, 0, unroll=4)
        add_looks(part, 0, pairs)

    sub = lax.broadcasted_iota(jnp.int32, (8, LANES), 0)
    lane = lax.broadcasted_iota(jnp.int32, (8, LANES), 1)
    low_half = sub < 4
    left = lane < 64
    group_zero = (lane & 32) == 0

    for part in range(parts):
        powers(part)
    for date in range(2):
        held = jnp.zeros((8, LANES), jnp.float32)
        for k, target in enumerate(targets):
            held = jnp.where(lane // looks_half == target, looks[2 * (pairs + k) + date], held)
        own_power[date] = held
        for side in range(2):
            own_rims[side, date] = own_power[date, pl.ds(3 * side, 2, stride=4)]
    power[pl.ds(2 * me, 2)] = own_power[...]

    back = []

    def send_powers():
        for k, target in enumerate(targets):
            if k < wide - 1:
                copy = pltpu.make_async_remote_copy(
                    src_ref=own_power,
                    dst_ref=power.at[pl.ds(2 * me, 2)],
                    send_sem=power_send.at[k],
                    recv_sem=power_recv.at[me],
                    device_id={"wide": target},
                )
                copy.start()
                back.append(copy)
            for side in range(2):
                copy = pltpu.make_async_remote_copy(
                    src_ref=own_rims.at[side],
                    dst_ref=rims.at[side, pl.ds(2 * me, 2)],
                    send_sem=rim_send.at[side, k],
                    recv_sem=rim_recv.at[side, me],
                    device_id={"wide": target, "narrow": (above, below)[side]},
                )
                copy.start()
                back.append(copy)

    for part in range(parts):
        if part == parts - 1:
            for copy in started:
                copy.wait_send()
            send_powers()
        work(part)

    for k, target in enumerate(targets):
        own = k == wide - 1
        for term in range(2):
            held = jnp.zeros((8, LANES), jnp.float32)
            for slot in range(PAIR_DEV):
                place = target * PAIR_DEV + slot
                value = looks[2 * place + term]
                turned = pltpu.roll(value, 4, 0)
                if slot < 2:
                    value = jnp.where(group_zero, value, turned)
                else:
                    value = jnp.where(group_zero, turned, value)
                here = (low_half if slot < 2 else ~low_half) & (left if slot % 2 == 0 else ~left)
                held = jnp.where(here, value, held)
            message[k, 8 * term : 8 * term + 8] = held
        for side in range(2):
            edges[k, side] = message[k, pl.ds(3 * side, 4, stride=4)]
        if own:
            got[me] = message[k]
        else:
            copy = pltpu.make_async_remote_copy(
                src_ref=message.at[k],
                dst_ref=got.at[me],
                send_sem=back_send.at[k],
                recv_sem=back_recv.at[me],
                device_id={"wide": target},
            )
            copy.start()
            back.append(copy)
        for side in range(2):
            copy = pltpu.make_async_remote_copy(
                src_ref=edges.at[k, side],
                dst_ref=got_edges.at[side, me],
                send_sem=edge_send.at[side, k],
                recv_sem=edge_recv.at[side, me],
                device_id={"wide": target, "narrow": (above, below)[side]},
            )
            copy.start()
            back.append(copy)

    for k, target in enumerate(targets):
        if k < wide - 1:
            pltpu.make_async_remote_copy(
                src_ref=own_power,
                dst_ref=power.at[pl.ds(2 * target, 2)],
                send_sem=power_send.at[k],
                recv_sem=power_recv.at[target],
                device_id={"wide": target},
            ).wait_recv()
        for side in range(2):
            pltpu.make_async_remote_copy(
                src_ref=own_rims.at[side],
                dst_ref=rims.at[side, pl.ds(2 * target, 2)],
                send_sem=rim_send.at[side, k],
                recv_sem=rim_recv.at[side, target],
                device_id={"wide": target, "narrow": (above, below)[side]},
            ).wait_recv()

    columns = wide * 64
    place = lax.broadcasted_iota(jnp.int32, (4, columns), 1)

    def box(field):
        rows = grown[field][0:4] + grown[field][1:5] + grown[field][2:6]
        before = jnp.where(place == 0, 0.0, pltpu.roll(rows, 1, 1))
        after = jnp.where(place == columns - 1, 0.0, pltpu.roll(rows, columns - 1, 1))
        return before + rows + after

    spare = jnp.zeros((2, LANES), jnp.float32)
    for slot in range(PAIR_DEV):
        chosen = owner_ref[me * PAIR_DEV + slot]
        for term in range(2):
            date = pair_ref[term, chosen]
            value = power[date]
            top = jnp.where(row == 0, 0.0, rims[1, date])
            bottom = jnp.where(row == narrow - 1, 0.0, rims[0, date])
            groups = [
                jnp.concatenate(
                    [top[g : g + 1], value[4 * g : 4 * g + 4], bottom[g : g + 1], spare], axis=0
                )
                for g in range(2)
            ]
            for tile in range(2):
                held = None
                for index in range(4):
                    e, g = index // 2, index % 2
                    shift = 32 * (e + g - 2 * tile) % LANES
                    moved = pltpu.roll(groups[g], shift, 1) if shift else groups[g]
                    if held is None:
                        held = moved
                    else:
                        held = jnp.where(lane // 32 == index, moved, held)
                grown[2 + term, slot, :, tile * LANES : (tile + 1) * LANES] = held
        below_line[slot] = jnp.sqrt(box((2, slot)) * box((3, slot)) + 1e-06)

    for k, target in enumerate(targets):
        if k < wide - 1:
            pltpu.make_async_remote_copy(
                src_ref=message.at[k],
                dst_ref=got.at[target],
                send_sem=back_send.at[k],
                recv_sem=back_recv.at[target],
                device_id={"wide": target},
            ).wait_recv()
        for side in range(2):
            pltpu.make_async_remote_copy(
                src_ref=edges.at[k, side],
                dst_ref=got_edges.at[side, target],
                send_sem=edge_send.at[side, k],
                recv_sem=edge_recv.at[side, target],
                device_id={"wide": target, "narrow": (above, below)[side]},
            ).wait_recv()

    def across(parts, parity):
        tiles = []
        first = lax.broadcasted_iota(jnp.int32, parts[0].shape, 1) < 64
        for i in range(0, wide, 2):
            one, two = parts[i], parts[i + 1]
            if parity == 0:
                tiles.append(jnp.where(first, one, pltpu.roll(two, 64, 1)))
            else:
                tiles.append(jnp.where(first, pltpu.roll(one, 64, 1), two))
        return jnp.concatenate(tiles, axis=1)

    for parity in range(2):
        top = across([got_edges[1, w] for w in range(wide)], parity)
        bottom = across([got_edges[0, w] for w in range(wide)], parity)
        top = jnp.where(row == 0, 0.0, top)
        bottom = jnp.where(row == narrow - 1, 0.0, bottom)
        for term in range(2):
            middle = across([got[w, 8 * term : 8 * term + 8] for w in range(wide)], parity)
            for upper in range(2):
                slot = 2 * upper + parity
                edge = 2 * term + upper
                grown[term, slot, 0:1] = top[edge : edge + 1]
                grown[term, slot, 1:5] = middle[4 * upper : 4 * upper + 4]
                grown[term, slot, 5:6] = bottom[edge : edge + 1]

    for slot in range(PAIR_DEV):
        boxed = [box((term, slot)) for term in range(2)]
        for term in range(2):
            inter_ref[term, slot] = grown[term, slot, 1:5] / (ML_ROWS * ML_COLS)
        magnitude = jnp.sqrt(boxed[0] * boxed[0] + boxed[1] * boxed[1])
        coh_ref[slot] = magnitude / below_line[slot]

    for copy in back:
        copy.wait_send()


def exchanged(slc, pair_list, owner):
    wide = lax.axis_size("wide")
    narrow = lax.axis_size("narrow")
    columns = slc.shape[3]
    half = columns // wide // 2
    widths = tuple(min(PART, half - i) for i in range(0, half, PART))
    pairs = owner.shape[0]
    dates = 2 * wide
    blocks = pairs + dates // 2
    bf16, f32 = jnp.bfloat16, jnp.float32
    scratch = [
        pltpu.VMEM((2, slc.shape[2], 2, columns), bf16),
        pltpu.VMEM((4, widths[0] // LANES, 2 * slc.shape[2], LANES), f32),
    ]
    scratch += [
        [pltpu.VMEM((wide - 1, 2, ML_ROWS, 16, n), bf16) for n in widths],
        [pltpu.VMEM((dates, ML_ROWS, 16, n), bf16) for n in widths],
        [pltpu.VMEM((blocks, 16, n), bf16) for n in widths],
        [pltpu.VMEM((blocks, 16, n), bf16) for n in widths],
    ]
    scratch += [
        pltpu.VMEM((2 * blocks, 8, LANES), f32),
        pltpu.VMEM((wide, 16, LANES), f32),
        pltpu.VMEM((wide, 2, 4, LANES), f32),
        pltpu.VMEM((wide, 16, LANES), f32),
        pltpu.VMEM((2, wide, 4, LANES), f32),
        pltpu.VMEM((2, 8, LANES), f32),
        pltpu.VMEM((2, 2, 2, LANES), f32),
        pltpu.VMEM((dates, 8, LANES), f32),
        pltpu.VMEM((2, dates, 2, LANES), f32),
        pltpu.VMEM((4, PAIR_DEV, 8, wide * 64), f32),
        pltpu.VMEM((PAIR_DEV, 4, wide * 64), f32),
        pltpu.SemaphoreType.DMA((wide,)),
        pltpu.SemaphoreType.DMA((len(widths), wide - 1)),
        pltpu.SemaphoreType.DMA((len(widths), wide)),
        pltpu.SemaphoreType.DMA((wide,)),
        pltpu.SemaphoreType.DMA((wide,)),
        pltpu.SemaphoreType.DMA((2, wide)),
        pltpu.SemaphoreType.DMA((2, wide)),
        pltpu.SemaphoreType.DMA((wide,)),
        pltpu.SemaphoreType.DMA((wide,)),
        pltpu.SemaphoreType.DMA((2, wide)),
        pltpu.SemaphoreType.DMA((2, wide)),
    ]
    look_rows = slc.shape[2] // ML_ROWS
    look_columns = columns // ML_COLS
    return pl.pallas_call(
        functools.partial(exchange_kernel, wide, narrow, half, widths),
        out_shape=(
            pltpu.VMEM((2, PAIR_DEV, look_rows, look_columns), f32),
            pltpu.VMEM((PAIR_DEV, look_rows, look_columns), f32),
        ),
        in_specs=[
            pl.BlockSpec(memory_space=pltpu.SMEM),
            pl.BlockSpec(memory_space=pltpu.SMEM),
            pl.BlockSpec(memory_space=pltpu.HBM),
        ],
        out_specs=(pl.BlockSpec(memory_space=pltpu.VMEM), pl.BlockSpec(memory_space=pltpu.VMEM)),
        scratch_shapes=scratch,
        compiler_params=pltpu.CompilerParams(
            collective_id=0, has_side_effects=True, vmem_limit_bytes=56 * 1024 * 1024
        ),
    )(*(pltpu.with_memory_space_constraint(x, pltpu.HBM) for x in (pair_list.T, owner, slc.transpose(0, 2, 1, 3))))


def solution(mesh):
    in_specs = (P(None, ("frames", "wide"), "narrow", None), P(), P())
    out_specs = (P(None, ("frames", "wide"), "narrow", None), P(("frames", "wide"), "narrow", None))

    def on_device(slc, pair_list, owner):
        wide, narrow = mesh.shape["wide"], mesh.shape["narrow"]
        tiled = slc.shape[3] == wide * 2 * ML_COLS * 32
        if tiled and narrow > 2 and wide == 4 and slc.shape[1:3] == (2, 4 * ML_ROWS):
            return exchanged(slc, pair_list, owner)
        return gathered(slc, pair_list, owner)

    return jax.shard_map(
        on_device, mesh=mesh, in_specs=in_specs, out_specs=out_specs, check_vma=False
    )
```

```python
import functools

import jax
import jax.numpy as jnp
from jax import lax
from jax.experimental import pallas as pl
from jax.experimental.pallas import tpu as pltpu
from jax.sharding import PartitionSpec as P

PAIR_DEV = 4
ML_ROWS = 5
ML_COLS = 20


def with_halo(block, sides, width):
    for axis, dim in sides:
        count = lax.axis_size(axis)
        forward = [(i, i + 1) for i in range(count - 1)]
        backward = [(target, source) for source, target in forward]
        low = lax.ppermute(
            lax.slice_in_dim(block, block.shape[dim] - width, None, axis=dim), axis, forward
        )
        high = lax.ppermute(lax.slice_in_dim(block, 0, width, axis=dim), axis, backward)
        block = jnp.concatenate([low, block, high], axis=dim)
    return block


def cross_terms(first, second):
    a0 = first[0].astype(jnp.float32)
    a1 = first[1].astype(jnp.float32)
    b0 = second[0].astype(jnp.float32)
    b1 = second[1].astype(jnp.float32)
    return jnp.stack([a0 * b0 + a1 * b1, a1 * b0 - a0 * b1, a0 * a0 + a1 * a1, b0 * b0 + b1 * b1])


def gathered(slc, pair_list, owner):
    pair_dev = PAIR_DEV
    look_rows = slc.shape[2] // ML_ROWS
    slots = lax.dynamic_slice_in_dim(owner, lax.axis_index("wide") * pair_dev, pair_dev)
    chosen = pair_list[slots]
    needed = jnp.concatenate([chosen[:, 0], chosen[:, 1]])
    piece = lax.all_gather(slc, "wide", axis=1, tiled=True)
    count = piece.shape[1]
    onehot = (needed[:, None] == jnp.arange(count, dtype=jnp.int32)[None, :]).astype(jnp.bfloat16)
    picked = jnp.einsum("sp,cprk->csrk", onehot, piece, preferred_element_type=jnp.float32)
    selected = picked.astype(jnp.bfloat16)
    terms = cross_terms(selected[:, :pair_dev], selected[:, pair_dev:])
    band = terms.shape[3]
    looked = terms.reshape(4, pair_dev, look_rows, ML_ROWS, band // ML_COLS, ML_COLS).sum(
        axis=(3, 5)
    )
    padded = with_halo(looked, (("narrow", 2),), 1)
    rowsum = padded[:, :, :-2] + padded[:, :, 1:-1] + padded[:, :, 2:]
    rowsum = jnp.pad(rowsum, ((0, 0), (0, 0), (0, 0), (1, 1)))
    boxed = rowsum[:, :, :, :-2] + rowsum[:, :, :, 1:-1] + rowsum[:, :, :, 2:]
    magnitude = jnp.sqrt(boxed[0] * boxed[0] + boxed[1] * boxed[1])
    coherence = magnitude / jnp.sqrt(boxed[2] * boxed[3] + 1e-06)
    interferogram = looked[:2] / (ML_ROWS * ML_COLS)
    return (interferogram, coherence)


LANES = 128
PART = 128


def split_terms(value):
    high = value.astype(jnp.bfloat16)
    return high, (value - high.astype(jnp.float32)).astype(jnp.bfloat16)


def exchange_kernel(
    wide, narrow, half, widths, pair_ref, owner_ref, slc_ref, inter_ref, coh_ref,
    pixels, stage, sends, recvs, highs, lows, looks, message, edges, got, got_edges,
    own_power, own_rims, power, rims, grown, below_line,
    load_sem, send_sem, recv_sem, back_send, back_recv, edge_send, edge_recv,
    power_send, power_recv, rim_send, rim_recv,
):
    me = lax.axis_index("wide")
    row = lax.axis_index("narrow")
    above = lax.rem(row + narrow - 1, narrow)
    below = lax.rem(row + 1, narrow)
    targets = [lax.rem(me + 2, wide), wide - 1 - me, me + 1 - 2 * lax.rem(me, 2), me]
    others = targets[:-1]
    parts = len(widths)
    pairs = owner_ref.shape[0]
    lines = slc_ref.shape[1]
    look_rows = lines // ML_ROWS

    loads = []
    for k, target in enumerate(targets):
        band = pl.ds(pl.multiple_of(target * (2 * half), LANES), 2 * half)
        load = pltpu.make_async_copy(
            slc_ref.at[:, :, :, band], pixels.at[:, :, :, band], load_sem.at[k]
        )
        load.start()
        loads.append(load)
    barrier = pltpu.get_barrier_semaphore()
    for target in others:
        pl.semaphore_signal(barrier, inc=1, device_id={"wide": target})
    for target in targets:
        for side in (above, below):
            pl.semaphore_signal(barrier, inc=1, device_id={"wide": target, "narrow": side})

    def pack(target, part, dst):
        width = widths[part]
        offset = sum(widths[:part])
        for comp in range(2):
            for group in range(2):
                column = pl.multiple_of(target * (2 * half) + (group * half + offset), LANES)
                for line in range(lines):
                    block = pixels[comp, line, :, pl.ds(column, width)].astype(jnp.float32)
                    for tile in range(width // LANES):
                        stage[comp * 2 + group, tile, 2 * line : 2 * line + 2] = block[
                            :, tile * LANES : (tile + 1) * LANES
                        ]
        for date in range(2):
            for line in range(ML_ROWS):
                for tile in range(width // LANES):
                    rows = [
                        stage[i, tile, pl.ds(2 * line + date, look_rows, stride=2 * ML_ROWS)]
                        for i in range(4)
                    ]
                    dst[date, line, :, tile * LANES : (tile + 1) * LANES] = jnp.concatenate(
                        rows, axis=0
                    ).astype(jnp.bfloat16)

    started = []

    def send(part):
        for k, target in enumerate(others):
            if part == 0:
                loads[k].wait()
            pack(target, part, sends[part].at[k])
            if part == 0 and k == 0:
                pl.semaphore_wait(barrier, 3 * wide - 1)
            copy = pltpu.make_async_remote_copy(
                src_ref=sends[part].at[k],
                dst_ref=recvs[part].at[pl.ds(2 * me, 2)],
                send_sem=send_sem.at[part, k],
                recv_sem=recv_sem.at[part, me],
                device_id={"wide": target},
            )
            copy.start()
            started.append(copy)

    for part in range(parts):
        send(part)
    loads[-1].wait()
    for part in range(parts):
        pack(me, part, recvs[part].at[pl.ds(2 * me, 2)])

    looks_half = half // ML_COLS

    def summer(part):
        width = widths[part]
        offset = sum(widths[:part])
        pixel = lax.broadcasted_iota(jnp.int32, (width, LANES), 0) + offset
        look = lax.broadcasted_iota(jnp.int32, (width, LANES), 1) & (looks_half - 1)
        first = look * ML_COLS
        return ((pixel >= first) & (pixel < first + ML_COLS)).astype(jnp.bfloat16)

    def add_looks(part, begin, end):
        width = widths[part]
        count = (end - begin) * 16
        spread = summer(part)
        summed = jnp.dot(
            highs[part][begin:end].reshape(count, width),
            spread,
            preferred_element_type=jnp.float32,
        ) + jnp.dot(
            lows[part][begin:end].reshape(count, width),
            spread,
            preferred_element_type=jnp.float32,
        )
        summed = summed.reshape(count // 8, 8, LANES)
        if part == 0:
            looks[2 * begin : 2 * end] = summed
        else:
            looks[2 * begin : 2 * end] += summed

    def powers(part):
        width = widths[part]
        for k in range(wide):
            both = []
            for date in range(2):
                total = jnp.zeros((8, width), jnp.float32)
                for line in range(ML_ROWS):
                    if k < wide - 1:
                        value = sends[part][k, date, line].astype(jnp.float32)
                    else:
                        value = recvs[part][2 * me + date, line].astype(jnp.float32)
                    total += value[:8] * value[:8] + value[8:] * value[8:]
                both.append(total)
            highs[part][pairs + k], lows[part][pairs + k] = split_terms(
                jnp.concatenate(both, axis=0)
            )
        add_looks(part, pairs, pairs + wide)

    def work(part):
        width = widths[part]
        recv = recvs[part]
        high, low = highs[part], lows[part]
        for k, target in enumerate(others):
            pltpu.make_async_remote_copy(
                src_ref=sends[part].at[k],
                dst_ref=recv.at[pl.ds(2 * target, 2)],
                send_sem=send_sem.at[part, k],
                recv_sem=recv_sem.at[part, target],
                device_id={"wide": target},
            ).wait_recv()

        def cross(slot, carry):
            chosen = owner_ref[slot]
            one, two = pair_ref[0, chosen], pair_ref[1, chosen]
            real = jnp.zeros((8, width), jnp.float32)
            imag = jnp.zeros((8, width), jnp.float32)
            for line in range(ML_ROWS):
                a = recv[one, line].astype(jnp.float32)
                b = recv[two, line].astype(jnp.float32)
                real += a[:8] * b[:8] + a[8:] * b[8:]
                imag += a[8:] * b[:8] - a[:8] * b[8:]
            high[slot], low[slot] = split_terms(jnp.concatenate([real, imag], axis=0))
            return carry

        lax.fori_loop(0, pairs, cross, 0, unroll=4)
        add_looks(part, 0, pairs)

    sub = lax.broadcasted_iota(jnp.int32, (8, LANES), 0)
    lane = lax.broadcasted_iota(jnp.int32, (8, LANES), 1)
    low_half = sub < 4
    left = lane < 64
    group_zero = (lane & 32) == 0

    for part in range(parts):
        powers(part)
    for date in range(2):
        held = jnp.zeros((8, LANES), jnp.float32)
        for k, target in enumerate(targets):
            held = jnp.where(lane // looks_half == target, looks[2 * (pairs + k) + date], held)
        own_power[date] = held
        for side in range(2):
            own_rims[side, date] = own_power[date, pl.ds(3 * side, 2, stride=4)]
    power[pl.ds(2 * me, 2)] = own_power[...]

    back = []

    def send_powers():
        for k, target in enumerate(targets):
            if k < wide - 1:
                copy = pltpu.make_async_remote_copy(
                    src_ref=own_power,
                    dst_ref=power.at[pl.ds(2 * me, 2)],
                    send_sem=power_send.at[k],
                    recv_sem=power_recv.at[me],
                    device_id={"wide": target},
                )
                copy.start()
                back.append(copy)
            for side in range(2):
                copy = pltpu.make_async_remote_copy(
                    src_ref=own_rims.at[side],
                    dst_ref=rims.at[side, pl.ds(2 * me, 2)],
                    send_sem=rim_send.at[side, k],
                    recv_sem=rim_recv.at[side, me],
                    device_id={"wide": target, "narrow": (above, below)[side]},
                )
                copy.start()
                back.append(copy)

    for part in range(parts):
        if part == parts - 1:
            for copy in started:
                copy.wait_send()
            send_powers()
        work(part)

    for k, target in enumerate(targets):
        own = k == wide - 1
        for term in range(2):
            held = jnp.zeros((8, LANES), jnp.float32)
            for slot in range(PAIR_DEV):
                place = target * PAIR_DEV + slot
                value = looks[2 * place + term]
                turned = pltpu.roll(value, 4, 0)
                if slot < 2:
                    value = jnp.where(group_zero, value, turned)
                else:
                    value = jnp.where(group_zero, turned, value)
                here = (low_half if slot < 2 else ~low_half) & (left if slot % 2 == 0 else ~left)
                held = jnp.where(here, value, held)
            message[k, 8 * term : 8 * term + 8] = held
        for side in range(2):
            edges[k, side] = message[k, pl.ds(3 * side, 4, stride=4)]
        if own:
            got[me] = message[k]
        else:
            copy = pltpu.make_async_remote_copy(
                src_ref=message.at[k],
                dst_ref=got.at[me],
                send_sem=back_send.at[k],
                recv_sem=back_recv.at[me],
                device_id={"wide": target},
            )
            copy.start()
            back.append(copy)
        for side in range(2):
            copy = pltpu.make_async_remote_copy(
                src_ref=edges.at[k, side],
                dst_ref=got_edges.at[side, me],
                send_sem=edge_send.at[side, k],
                recv_sem=edge_recv.at[side, me],
                device_id={"wide": target, "narrow": (above, below)[side]},
            )
            copy.start()
            back.append(copy)

    for k, target in enumerate(targets):
        if k < wide - 1:
            pltpu.make_async_remote_copy(
                src_ref=own_power,
                dst_ref=power.at[pl.ds(2 * target, 2)],
                send_sem=power_send.at[k],
                recv_sem=power_recv.at[target],
                device_id={"wide": target},
            ).wait_recv()
        for side in range(2):
            pltpu.make_async_remote_copy(
                src_ref=own_rims.at[side],
                dst_ref=rims.at[side, pl.ds(2 * target, 2)],
                send_sem=rim_send.at[side, k],
                recv_sem=rim_recv.at[side, target],
                device_id={"wide": target, "narrow": (above, below)[side]},
            ).wait_recv()

    columns = wide * 64
    place = lax.broadcasted_iota(jnp.int32, (4, columns), 1)

    def box(field):
        rows = grown[field][0:4] + grown[field][1:5] + grown[field][2:6]
        before = jnp.where(place == 0, 0.0, pltpu.roll(rows, 1, 1))
        after = jnp.where(place == columns - 1, 0.0, pltpu.roll(rows, columns - 1, 1))
        return before + rows + after

    spare = jnp.zeros((2, LANES), jnp.float32)
    for slot in range(PAIR_DEV):
        chosen = owner_ref[me * PAIR_DEV + slot]
        for term in range(2):
            date = pair_ref[term, chosen]
            value = power[date]
            top = jnp.where(row == 0, 0.0, rims[1, date])
            bottom = jnp.where(row == narrow - 1, 0.0, rims[0, date])
            groups = [
                jnp.concatenate(
                    [top[g : g + 1], value[4 * g : 4 * g + 4], bottom[g : g + 1], spare], axis=0
                )
                for g in range(2)
            ]
            for tile in range(2):
                held = None
                for index in range(4):
                    e, g = index // 2, index % 2
                    shift = 32 * (e + g - 2 * tile) % LANES
                    moved = pltpu.roll(groups[g], shift, 1) if shift else groups[g]
                    if held is None:
                        held = moved
                    else:
                        held = jnp.where(lane // 32 == index, moved, held)
                grown[2 + term, slot, :, tile * LANES : (tile + 1) * LANES] = held
        below_line[slot] = jnp.sqrt(box((2, slot)) * box((3, slot)) + 1e-06)

    for k, target in enumerate(targets):
        if k < wide - 1:
            pltpu.make_async_remote_copy(
                src_ref=message.at[k],
                dst_ref=got.at[target],
                send_sem=back_send.at[k],
                recv_sem=back_recv.at[target],
                device_id={"wide": target},
            ).wait_recv()
        for side in range(2):
            pltpu.make_async_remote_copy(
                src_ref=edges.at[k, side],
                dst_ref=got_edges.at[side, target],
                send_sem=edge_send.at[side, k],
                recv_sem=edge_recv.at[side, target],
                device_id={"wide": target, "narrow": (above, below)[side]},
            ).wait_recv()

    def across(parts, parity):
        tiles = []
        first = lax.broadcasted_iota(jnp.int32, parts[0].shape, 1) < 64
        for i in range(0, wide, 2):
            one, two = parts[i], parts[i + 1]
            if parity == 0:
                tiles.append(jnp.where(first, one, pltpu.roll(two, 64, 1)))
            else:
                tiles.append(jnp.where(first, pltpu.roll(one, 64, 1), two))
        return jnp.concatenate(tiles, axis=1)

    for parity in range(2):
        top = across([got_edges[1, w] for w in range(wide)], parity)
        bottom = across([got_edges[0, w] for w in range(wide)], parity)
        top = jnp.where(row == 0, 0.0, top)
        bottom = jnp.where(row == narrow - 1, 0.0, bottom)
        for term in range(2):
            middle = across([got[w, 8 * term : 8 * term + 8] for w in range(wide)], parity)
            for upper in range(2):
                slot = 2 * upper + parity
                edge = 2 * term + upper
                grown[term, slot, 0:1] = top[edge : edge + 1]
                grown[term, slot, 1:5] = middle[4 * upper : 4 * upper + 4]
                grown[term, slot, 5:6] = bottom[edge : edge + 1]

    for slot in range(PAIR_DEV):
        boxed = [box((term, slot)) for term in range(2)]
        for term in range(2):
            inter_ref[term, slot] = grown[term, slot, 1:5] / (ML_ROWS * ML_COLS)
        magnitude = jnp.sqrt(boxed[0] * boxed[0] + boxed[1] * boxed[1])
        coh_ref[slot] = magnitude / below_line[slot]

    for copy in back:
        copy.wait_send()


def exchanged(slc, pair_list, owner):
    wide = lax.axis_size("wide")
    narrow = lax.axis_size("narrow")
    columns = slc.shape[3]
    half = columns // wide // 2
    widths = tuple(min(PART, half - i) for i in range(0, half, PART))
    pairs = owner.shape[0]
    dates = 2 * wide
    blocks = pairs + dates // 2
    bf16, f32 = jnp.bfloat16, jnp.float32
    scratch = [
        pltpu.VMEM((2, slc.shape[2], 2, columns), bf16),
        pltpu.VMEM((4, widths[0] // LANES, 2 * slc.shape[2], LANES), f32),
    ]
    scratch += [
        [pltpu.VMEM((wide - 1, 2, ML_ROWS, 16, n), bf16) for n in widths],
        [pltpu.VMEM((dates, ML_ROWS, 16, n), bf16) for n in widths],
        [pltpu.VMEM((blocks, 16, n), bf16) for n in widths],
        [pltpu.VMEM((blocks, 16, n), bf16) for n in widths],
    ]
    scratch += [
        pltpu.VMEM((2 * blocks, 8, LANES), f32),
        pltpu.VMEM((wide, 16, LANES), f32),
        pltpu.VMEM((wide, 2, 4, LANES), f32),
        pltpu.VMEM((wide, 16, LANES), f32),
        pltpu.VMEM((2, wide, 4, LANES), f32),
        pltpu.VMEM((2, 8, LANES), f32),
        pltpu.VMEM((2, 2, 2, LANES), f32),
        pltpu.VMEM((dates, 8, LANES), f32),
        pltpu.VMEM((2, dates, 2, LANES), f32),
        pltpu.VMEM((4, PAIR_DEV, 8, wide * 64), f32),
        pltpu.VMEM((PAIR_DEV, 4, wide * 64), f32),
        pltpu.SemaphoreType.DMA((wide,)),
        pltpu.SemaphoreType.DMA((len(widths), wide - 1)),
        pltpu.SemaphoreType.DMA((len(widths), wide)),
        pltpu.SemaphoreType.DMA((wide,)),
        pltpu.SemaphoreType.DMA((wide,)),
        pltpu.SemaphoreType.DMA((2, wide)),
        pltpu.SemaphoreType.DMA((2, wide)),
        pltpu.SemaphoreType.DMA((wide,)),
        pltpu.SemaphoreType.DMA((wide,)),
        pltpu.SemaphoreType.DMA((2, wide)),
        pltpu.SemaphoreType.DMA((2, wide)),
    ]
    look_rows = slc.shape[2] // ML_ROWS
    look_columns = columns // ML_COLS
    return pl.pallas_call(
        functools.partial(exchange_kernel, wide, narrow, half, widths),
        out_shape=(
            pltpu.VMEM((2, PAIR_DEV, look_rows, look_columns), f32),
            pltpu.VMEM((PAIR_DEV, look_rows, look_columns), f32),
        ),
        in_specs=[
            pl.BlockSpec(memory_space=pltpu.SMEM),
            pl.BlockSpec(memory_space=pltpu.SMEM),
            pl.BlockSpec(memory_space=pltpu.HBM),
        ],
        out_specs=(pl.BlockSpec(memory_space=pltpu.VMEM), pl.BlockSpec(memory_space=pltpu.VMEM)),
        scratch_shapes=scratch,
        compiler_params=pltpu.CompilerParams(
            collective_id=0, has_side_effects=True, vmem_limit_bytes=56 * 1024 * 1024
        ),
    )(*(pltpu.with_memory_space_constraint(x, pltpu.HBM) for x in (pair_list.T, owner, slc.transpose(0, 2, 1, 3))))


def solution(mesh):
    in_specs = (P(None, ("frames", "wide"), "narrow", None), P(), P())
    out_specs = (P(None, ("frames", "wide"), "narrow", None), P(("frames", "wide"), "narrow", None))

    def on_device(slc, pair_list, owner):
        wide, narrow = mesh.shape["wide"], mesh.shape["narrow"]
        tiled = slc.shape[3] == wide * 2 * ML_COLS * 32
        if tiled and narrow > 2 and wide == 4 and slc.shape[1:3] == (2, 4 * ML_ROWS):
            return exchanged(slc, pair_list, owner)
        return gathered(slc, pair_list, owner)

    return jax.shard_map(
        on_device, mesh=mesh, in_specs=in_specs, out_specs=out_specs, check_vma=False
    )
```
